32 devices in a mesh: groups: 2 (over x), dp: 16 (over z, y, core).
Axes of the slice: x: 2, y: 2, z: 4, core: 2. Of those that a mesh axis runs over, the one named last changes fastest.
Arguments:
- embeddings: bfloat16 [16384, 1152], P(('groups', 'dp')), parts along dimension 0, may hold values from -600 to 600
- labels: int32 [16384], P(('groups', 'dp')), parts along dimension 0, may hold values from 0 to 31, as said below
Outputs:
- best_match: float32 [16384], P(('groups', 'dp')), parts along dimension 0
The draws below stay inside these ranges and needn't reach their ends.
There are 2 independent parts, one for each index of `groups`. The reference program is written for one: setup_inputs(seed, part) draws one part's arguments, and reference() takes and returns one part's arrays. A program takes and returns all parts, laid end to end along the dimension named above; each array names one. Nothing has to cross between parts.
Inputs may be any that keep to these rules, and one draw needn't show every extreme that they name: `labels`: each device's 512 rows name each cluster at most 32 times, and on every device some cluster exactly 32 times.
All inputs are finite; a program needn't handle non-finite values.
Results may differ from the reference program's by a relative error of at most 0.00045.
Values may be sent and summed in bfloat16 or wider, within the bound.
A program may use at most 128 MiB of HBM per device.

```python
import jax
import jax.numpy as jnp
from jax import lax

D = 1152
CAP = 32
CLUSTERS = 32
ROWS_DEV = 512
ROWS = 8192
N_DP = 16


def cluster_labels(key):
    key = jax.random.fold_in(key, 11)
    slots = CLUSTERS * CAP
    bias_key, device_key = jax.random.split(key)
    bias = jax.random.randint(bias_key, (CLUSTERS,), 0, 1536)

    def one_device(dkey):
        first, second, third = jax.random.split(dkey, 3)
        slot_ids = jnp.arange(slots, dtype=jnp.int32)
        holder = slot_ids // CAP
        chosen = jax.random.randint(first, (), 0, CLUSTERS)
        base = jax.random.randint(second, (slots,), 0, 1024) + bias[holder] + jnp.where(holder == chosen, 4096, 0)
        score = base * slots + slot_ids
        top_scores, picked = lax.top_k(score, ROWS_DEV)
        named = picked // CAP
        return named[jax.random.permutation(third, ROWS_DEV)]
    keys = jax.random.split(device_key, N_DP)
    return jax.vmap(one_device)(keys).reshape(-1).astype(jnp.int32)


def draw_labels(key, part):
    return cluster_labels(key)


def draw_embeddings(key, part):
    named = cluster_labels(key)
    key = jax.random.fold_in(key, 5)
    keys = jax.random.split(key, 7)
    centers = jax.random.normal(keys[0], (CLUSTERS, D), jnp.float32)
    subcenters = jax.random.normal(keys[1], (CLUSTERS * 4, D), jnp.float32)
    which = jax.random.randint(keys[2], (ROWS,), 0, 4)
    noise = jax.random.normal(keys[3], (ROWS, D), jnp.float32)
    strength = jnp.exp(jax.random.uniform(keys[4], (ROWS, 1), jnp.float32, -1.2, 1.2))
    mixing = jnp.exp(jax.random.uniform(keys[5], (ROWS, 1), jnp.float32, -1.0, 1.5))
    scale = jnp.exp(jax.random.uniform(keys[6], (ROWS, 1), jnp.float32, -1.0, 1.0))
    rows = strength * centers[named] + mixing * subcenters[named * 4 + which] + noise
    return (jnp.clip(rows, -40.0, 40.0) * scale).astype(jnp.bfloat16)


def setup_inputs(seed: int = 0, part: int = 0) -> dict:
    key_list = jax.random.split(jax.random.key(seed), 3)
    part_keys = jax.random.split(jax.random.fold_in(key_list[2], part), 3)
    embeddings = draw_embeddings(jax.random.fold_in(jax.random.fold_in(key_list[2], part), 71), part)
    labels = draw_labels(jax.random.fold_in(jax.random.fold_in(key_list[2], part), 71), part)
    return dict(embeddings=embeddings, labels=labels)


def reference(embeddings, labels):
    wide = embeddings.astype(jnp.float32)
    unit = (wide * lax.rsqrt(lax.optimization_barrier(jnp.sum(wide * wide, axis=1, keepdims=True)) + 1e-06)).astype(jnp.bfloat16)
    order = jnp.argsort(labels, stable=True).astype(jnp.int32)
    sorted_labels = labels[order].astype(jnp.int32)
    names = jnp.arange(CLUSTERS, dtype=jnp.int32)
    sizes = lax.optimization_barrier(jnp.sum((labels[:, None] == names[None, :]).astype(jnp.int32), axis=0))
    offsets = (jnp.cumsum(sizes) - sizes).astype(jnp.int32)
    span = N_DP * CAP
    padded = jnp.concatenate([unit[order], jnp.zeros((span, unit.shape[1]), jnp.bfloat16)], axis=0)
    places = jnp.arange(span, dtype=jnp.int32)

    def per_cluster(cluster):
        start = offsets[cluster]
        block = lax.dynamic_slice_in_dim(padded, start, span, 0)
        scores = jnp.dot(block, block.T, preferred_element_type=jnp.float32)
        keep = (places[None, :] < places[:, None]) & (places[None, :] < sizes[cluster])
        return lax.optimization_barrier(jnp.max(jnp.where(keep, scores, -1.0), axis=1))
    table = lax.map(per_cluster, names)
    local = (jnp.arange(ROWS, dtype=jnp.int32) - offsets[sorted_labels]).astype(jnp.int32)
    best_sorted = table[sorted_labels, local]
    return jnp.zeros((ROWS,), jnp.float32).at[order].set(best_sorted)
```

```python
import functools

import jax
import jax.numpy as jnp
from jax import lax
from jax.experimental import pallas as pl
from jax.experimental.pallas import tpu as pltpu
from jax.sharding import PartitionSpec as P

CAP = 32
CL_DEV = 2
MESH = pl.DeviceIdType.MESH
SEND = CAP * CL_DEV
EMPTY = 2.0


def flip(me, k, n):
    total = 0
    bit = 1
    while bit < n:
        have = (me // bit) % 2
        total = total + ((1 - have) if (k // bit) % 2 else have) * bit
        bit *= 2
    return total


def kernel(n, rows, emb_ref, lab_ref, out_ref, unit, packed, got, mine, back, send_sem, recv_sem, bsend_sem, brecv_sem, own_sem):
    me = lax.axis_index("dp")
    group = lax.axis_index("groups")
    region = n * CAP
    strips = region // 128

    barrier = pltpu.get_barrier_semaphore()
    for k in range(1, n):
        pl.semaphore_signal(barrier, inc=1, device_id=(group, flip(me, k, n)), device_id_type=MESH)

    wide = emb_ref[...].astype(jnp.float32)
    unit[...] = (wide * lax.rsqrt(jnp.sum(wide * wide, axis=1, keepdims=True) + 1e-06)).astype(jnp.bfloat16)

    label = lab_ref[...]
    onehot = lax.broadcasted_iota(jnp.int32, (n * CL_DEV, rows), 0) == label
    before = lax.broadcasted_iota(jnp.int32, (rows, rows), 0) < lax.broadcasted_iota(jnp.int32, (rows, rows), 1)
    ranks = jnp.dot(
        onehot.astype(jnp.bfloat16), before.astype(jnp.bfloat16), preferred_element_type=jnp.float32
    )
    rank = jnp.sum(jnp.where(onehot, ranks, 0.0), axis=0, keepdims=True).astype(jnp.int32)
    position = label * CAP + rank

    per = min(4, n)
    width = emb_ref.shape[1]
    slot = lax.broadcasted_iota(jnp.int32, (SEND, rows), 0)
    first_lane = lax.broadcasted_iota(jnp.int32, (per * SEND, 128), 1) == 0
    copies = {}
    for chunk in reversed(range(n // per)):
        picks = []
        for k in range(chunk * per, (chunk + 1) * per):
            picks.append((position - flip(me, k, n) * SEND) == slot)
        pick = jnp.concatenate([p.astype(jnp.float32) for p in picks], axis=0)
        used = jnp.sum(pick, axis=1, keepdims=True)
        block = jnp.dot(pick.astype(jnp.bfloat16), unit[...], preferred_element_type=jnp.float32)
        head = jnp.where(first_lane, block[:, :128] + EMPTY * (1.0 - used), block[:, :128])
        at = pl.ds(chunk * per * SEND, per * SEND)
        packed[at, :128] = head.astype(jnp.bfloat16)
        packed[at, 128:] = block[:, 128:].astype(jnp.bfloat16)
        if chunk == n // per - 1:
            pl.semaphore_wait(barrier, n - 1)
        for k in reversed(range(chunk * per, (chunk + 1) * per)):
            src = packed.at[pl.ds(k * SEND, SEND)]
            if k == 0:
                copy = pltpu.make_async_copy(src, got.at[me], own_sem)
            else:
                copy = pltpu.make_async_remote_copy(
                    src_ref=src,
                    dst_ref=got.at[me],
                    send_sem=send_sem.at[k],
                    recv_sem=recv_sem.at[k],
                    device_id=(group, flip(me, k, n)),
                    device_id_type=MESH,
                )
            copy.start()
            copies[k] = copy
    copies[0].wait()
    for k in range(1, n):
        copies[k].wait_recv()

    block = min(256, region)
    per_block = block // CAP
    key_place = lax.broadcasted_iota(jnp.int32, (block, block), 0)
    query_place = lax.broadcasted_iota(jnp.int32, (block, block), 1)
    for c in range(CL_DEV):
        part = pl.ds(c * CAP, CAP)
        for qb in range(region // block):
            query = got[pl.ds(qb * per_block, per_block), part, :].reshape(block, width)
            best = jnp.full((1, block), -1.0, jnp.float32)
            for kb in range(qb + 1):
                keys = got[pl.ds(kb * per_block, per_block), part, :].reshape(block, width)
                scores = lax.dot_general(
                    keys, query, (((1,), (1,)), ((), ())), preferred_element_type=jnp.float32
                )
                keep = keys[:, :1].astype(jnp.float32) < 1.5
                if kb == qb:
                    keep = keep & (key_place < query_place)
                best = jnp.maximum(best, jnp.max(jnp.where(keep, scores, -1.0), axis=0, keepdims=True))
            for part_of in range(block // 128):
                mine[pl.ds(c * strips + qb * (block // 128) + part_of, 1), :] = best[
                    :, part_of * 128 : (part_of + 1) * 128
                ]

    returns = []
    for k in reversed(range(1, n)):
        copy = pltpu.make_async_remote_copy(
            src_ref=mine,
            dst_ref=back.at[me],
            send_sem=bsend_sem.at[k],
            recv_sem=brecv_sem.at[k],
            device_id=(group, flip(me, k, n)),
            device_id_type=MESH,
        )
        copy.start()
        returns.append(copy)
    own = pltpu.make_async_copy(mine, back.at[me], own_sem)
    own.start()
    own.wait()
    for k in range(1, n):
        copies[k].wait_send()
    for copy in returns:
        copy.wait()

    strip = (me * CAP) // 128
    lane = (me * CAP) % 128
    home = lax.broadcasted_iota(jnp.int32, (n, rows), 0) * CL_DEV
    spread = jnp.zeros((128, rows), jnp.float32)
    for c in range(CL_DEV):
        table = back[:, pl.ds(c * strips + strip, 1), :].reshape(n, 128)
        spread = spread + lax.dot_general(
            table,
            ((home + c) == label).astype(jnp.float32),
            (((0,), (0,)), ((), ())),
            preferred_element_type=jnp.float32,
            precision=lax.Precision.HIGHEST,
        )
    place = lax.broadcasted_iota(jnp.int32, (128, rows), 0) == (rank + lane)
    out_ref[...] = jnp.sum(jnp.where(place, spread, 0.0), axis=0, keepdims=True)


def solution(mesh):
    n = mesh.shape["dp"]

    def local(embeddings, labels):
        rows, width = embeddings.shape
        tile = (CL_DEV * n * CAP // 128, 128)
        best = pl.pallas_call(
            functools.partial(kernel, n, rows),
            out_shape=jax.ShapeDtypeStruct((1, rows), jnp.float32),
            in_specs=[pl.BlockSpec(memory_space=pltpu.VMEM)] * 2,
            out_specs=pl.BlockSpec(memory_space=pltpu.VMEM),
            scratch_shapes=[
                pltpu.VMEM((rows, width), jnp.bfloat16),
                pltpu.VMEM((n * SEND, width), jnp.bfloat16),
                pltpu.VMEM((n, SEND, width), jnp.bfloat16),
                pltpu.VMEM(tile, jnp.float32),
                pltpu.VMEM((n,) + tile, jnp.float32),
                pltpu.SemaphoreType.DMA((n,)),
                pltpu.SemaphoreType.DMA((n,)),
                pltpu.SemaphoreType.DMA((n,)),
                pltpu.SemaphoreType.DMA((n,)),
                pltpu.SemaphoreType.DMA,
            ],
            compiler_params=pltpu.CompilerParams(
                collective_id=0, has_side_effects=True, vmem_limit_bytes=56 * 1024 * 1024
            ),
        )(embeddings, labels.reshape(1, rows))
        return best.reshape(rows)

    in_specs = (P(("groups", "dp"), None), P(("groups", "dp")))
    return jax.shard_map(local, mesh=mesh, in_specs=in_specs, out_specs=P(("groups", "dp")), check_vma=False)
```

```python
import functools

import jax
import jax.numpy as jnp
from jax import lax
from jax.experimental import pallas as pl
from jax.experimental.pallas import tpu as pltpu
from jax.sharding import PartitionSpec as P

CAP = 32
CL_DEV = 2
MESH = pl.DeviceIdType.MESH
SEND = CAP * CL_DEV
EMPTY = 2.0
PER = 4


def flip(me, k, n):
    total = 0
    bit = 1
    while bit < n:
        have = (me // bit) % 2
        total = total + ((1 - have) if (k // bit) % 2 else have) * bit
        bit *= 2
    return total


def kernel(n, rows, emb_ref, lab_ref, out_ref, unit, packed, got, mine, back, send_sem, recv_sem, bsend_sem, brecv_sem, own_sem):
    me = lax.axis_index("dp")
    group = lax.axis_index("groups")
    region = n * CAP
    strips = region // 128

    barrier = pltpu.get_barrier_semaphore()
    for k in range(1, n):
        pl.semaphore_signal(barrier, inc=1, device_id=(group, flip(me, k, n)), device_id_type=MESH)

    wide = emb_ref[...].astype(jnp.float32)
    unit[...] = (wide * lax.rsqrt(jnp.sum(wide * wide, axis=1, keepdims=True) + 1e-06)).astype(jnp.bfloat16)

    label = lab_ref[...]
    onehot = lax.broadcasted_iota(jnp.int32, (n * CL_DEV, rows), 0) == label
    before = lax.broadcasted_iota(jnp.int32, (rows, rows), 0) < lax.broadcasted_iota(jnp.int32, (rows, rows), 1)
    ranks = jnp.dot(
        onehot.astype(jnp.bfloat16), before.astype(jnp.bfloat16), preferred_element_type=jnp.float32
    )
    rank = jnp.sum(jnp.where(onehot, ranks, 0.0), axis=0, keepdims=True).astype(jnp.int32)
    position = label * CAP + rank

    width = emb_ref.shape[1]
    groups = n // PER
    half = groups // 2
    slot = lax.broadcasted_iota(jnp.int32, (SEND, rows), 0)
    first_lane = lax.broadcasted_iota(jnp.int32, (PER * SEND, 128), 1) == 0
    copies = {}
    for chunk in [half] + list(range(half)) + list(range(half + 1, groups)):
        mates = range(chunk * PER, (chunk + 1) * PER)
        picks = [(position - flip(me, k, n) * SEND) == slot for k in mates]
        pick = jnp.concatenate([p.astype(jnp.float32) for p in picks], axis=0)
        used = jnp.sum(pick, axis=1, keepdims=True)
        block = jnp.dot(pick.astype(jnp.bfloat16), unit[...], preferred_element_type=jnp.float32)
        head = jnp.where(first_lane, block[:, :128] + EMPTY * (1.0 - used), block[:, :128])
        at = pl.ds(chunk * PER * SEND, PER * SEND)
        packed[at, :128] = head.astype(jnp.bfloat16)
        packed[at, 128:] = block[:, 128:].astype(jnp.bfloat16)
        if chunk == half:
            pl.semaphore_wait(barrier, n - 1)
        for k in mates:
            src = packed.at[pl.ds(k * SEND, SEND)]
            if k == 0:
                copies[k] = pltpu.make_async_copy(src, got.at[me], own_sem)
            else:
                copies[k] = pltpu.make_async_remote_copy(
                    src_ref=src,
                    dst_ref=got.at[me],
                    send_sem=send_sem.at[k],
                    recv_sem=recv_sem.at[k],
                    device_id=(group, flip(me, k, n)),
                    device_id_type=MESH,
                )
            copies[k].start()

    mine[...] = jnp.full(mine.shape, -1.0, jnp.float32)
    span = PER * CAP
    earlier = lax.broadcasted_iota(jnp.int32, (span, span), 0) < lax.broadcasted_iota(jnp.int32, (span, span), 1)
    my_group = me // PER
    for chunk in range(groups):
        for k in range(chunk * PER, (chunk + 1) * PER):
            if k == 0:
                copies[k].wait()
            else:
                copies[k].wait_recv()
        new = flip(my_group, chunk, groups)
        for other in range(chunk + 1):
            old = flip(my_group, other, groups)
            if other == chunk:
                low, high = new, new
            else:
                top = 1 << ((chunk ^ other).bit_length() - 1)
                later = (new // top) % 2
                low = new * (1 - later) + old * later
                high = new * later + old * (1 - later)
            for c in range(CL_DEV):
                part = pl.ds(c * CAP, CAP)
                keys = got[pl.ds(low * PER, PER), part, :].reshape(span, width)
                query = got[pl.ds(high * PER, PER), part, :].reshape(span, width)
                scores = lax.dot_general(
                    keys, query, (((1,), (1,)), ((), ())), preferred_element_type=jnp.float32
                )
                keep = keys[:, :1].astype(jnp.float32) < 1.5
                if other == chunk:
                    keep = keep & earlier
                best = jnp.max(jnp.where(keep, scores, -1.0), axis=0, keepdims=True)
                line = pl.ds(c * strips + high, 1)
                mine[line, :] = jnp.maximum(mine[line, :], best)

    returns = []
    for k in reversed(range(1, n)):
        copy = pltpu.make_async_remote_copy(
            src_ref=mine,
            dst_ref=back.at[me],
            send_sem=bsend_sem.at[k],
            recv_sem=brecv_sem.at[k],
            device_id=(group, flip(me, k, n)),
            device_id_type=MESH,
        )
        copy.start()
        returns.append(copy)
    own = pltpu.make_async_copy(mine, back.at[me], own_sem)
    own.start()
    own.wait()
    for k in range(1, n):
        copies[k].wait_send()
    for copy in returns:
        copy.wait()

    strip = (me * CAP) // 128
    lane = (me * CAP) % 128
    home = lax.broadcasted_iota(jnp.int32, (n, rows), 0) * CL_DEV
    spread = jnp.zeros((128, rows), jnp.float32)
    for c in range(CL_DEV):
        table = back[:, pl.ds(c * strips + strip, 1), :].reshape(n, 128)
        spread = spread + lax.dot_general(
            table,
            ((home + c) == label).astype(jnp.float32),
            (((0,), (0,)), ((), ())),
            preferred_element_type=jnp.float32,
            precision=lax.Precision.HIGHEST,
        )
    place = lax.broadcasted_iota(jnp.int32, (128, rows), 0) == (rank + lane)
    out_ref[...] = jnp.sum(jnp.where(place, spread, 0.0), axis=0, keepdims=True)


def solution(mesh):
    n = mesh.shape["dp"]

    def local(embeddings, labels):
        rows, width = embeddings.shape
        tile = (CL_DEV * n * CAP // 128, 128)
        best = pl.pallas_call(
            functools.partial(kernel, n, rows),
            out_shape=jax.ShapeDtypeStruct((1, rows), jnp.float32),
            in_specs=[pl.BlockSpec(memory_space=pltpu.VMEM)] * 2,
            out_specs=pl.BlockSpec(memory_space=pltpu.VMEM),
            scratch_shapes=[
                pltpu.VMEM((rows, width), jnp.bfloat16),
                pltpu.VMEM((n * SEND, width), jnp.bfloat16),
                pltpu.VMEM((n, SEND, width), jnp.bfloat16),
                pltpu.VMEM(tile, jnp.float32),
                pltpu.VMEM((n,) + tile, jnp.float32),
                pltpu.SemaphoreType.DMA((n,)),
                pltpu.SemaphoreType.DMA((n,)),
                pltpu.SemaphoreType.DMA((n,)),
                pltpu.SemaphoreType.DMA((n,)),
                pltpu.SemaphoreType.DMA,
            ],
            compiler_params=pltpu.CompilerParams(
                collective_id=0, has_side_effects=True, vmem_limit_bytes=56 * 1024 * 1024
            ),
        )(embeddings, labels.reshape(1, rows))
        return jnp.maximum(best.reshape(rows), -1.0)

    in_specs = (P(("groups", "dp"), None), P(("groups", "dp")))
    return jax.shard_map(local, mesh=mesh, in_specs=in_specs, out_specs=P(("groups", "dp")), check_vma=False)
```

```python
import functools

import jax
import jax.numpy as jnp
from jax import lax
from jax.experimental import pallas as pl
from jax.experimental.pallas import tpu as pltpu
from jax.sharding import PartitionSpec as P

CAP = 32
CL_DEV = 2
MESH = pl.DeviceIdType.MESH
SEND = CAP * CL_DEV
EMPTY = 32768.0
PER = 4


def flip(me, k, n):
    total = 0
    bit = 1
    while bit < n:
        have = (me // bit) % 2
        total = total + ((1 - have) if (k // bit) % 2 else have) * bit
        bit *= 2
    return total


def kernel(n, rows, emb_ref, lab_ref, out_ref, packed, got, mine, back, send_sem, recv_sem, bsend_sem, brecv_sem, own_sem):
    me = lax.axis_index("dp")
    group = lax.axis_index("groups")

    barrier = pltpu.get_barrier_semaphore()
    for k in range(1, n):
        pl.semaphore_signal(barrier, inc=1, device_id=(group, flip(me, k, n)), device_id_type=MESH)

    label = lab_ref[...]
    onehot = lax.broadcasted_iota(jnp.int32, (n * CL_DEV, rows), 0) == label
    before = lax.broadcasted_iota(jnp.int32, (rows, rows), 0) < lax.broadcasted_iota(jnp.int32, (rows, rows), 1)
    ranks = jnp.dot(
        onehot.astype(jnp.bfloat16), before.astype(jnp.bfloat16), preferred_element_type=jnp.float32
    )
    rank = jnp.sum(jnp.where(onehot, ranks, 0.0), axis=0, keepdims=True).astype(jnp.int32)
    position = label * CAP + rank

    width = emb_ref.shape[1]
    groups = n // PER
    half = groups // 2
    slot = lax.broadcasted_iota(jnp.int32, (SEND, rows), 0)
    first_lane = lax.broadcasted_iota(jnp.int32, (PER * SEND, 128), 1) == 0
    copies = {}
    for chunk in [half] + list(range(half)) + list(range(half + 1, groups)):
        mates = range(chunk * PER, (chunk + 1) * PER)
        picks = [(position - flip(me, k, n) * SEND) == slot for k in mates]
        pick = jnp.concatenate([p.astype(jnp.float32) for p in picks], axis=0)
        used = jnp.sum(pick, axis=1, keepdims=True)
        block = jnp.dot(pick.astype(jnp.bfloat16), emb_ref[...], preferred_element_type=jnp.float32)
        head = jnp.where(first_lane, block[:, :128] + EMPTY * (1.0 - used), block[:, :128])
        at = pl.ds(chunk * PER * SEND, PER * SEND)
        packed[at, :128] = head.astype(jnp.bfloat16)
        packed[at, 128:] = block[:, 128:].astype(jnp.bfloat16)
        if chunk == half:
            pl.semaphore_wait(barrier, n - 1)
        for k in mates:
            src = packed.at[pl.ds(k * SEND, SEND)]
            if k == 0:
                copies[k] = pltpu.make_async_copy(src, got.at[me], own_sem)
            else:
                copies[k] = pltpu.make_async_remote_copy(
                    src_ref=src,
                    dst_ref=got.at[me],
                    send_sem=send_sem.at[k],
                    recv_sem=recv_sem.at[k],
                    device_id=(group, flip(me, k, n)),
                    device_id_type=MESH,
                )
            copies[k].start()

    mine[...] = jnp.full(mine.shape, -1.0, jnp.float32)
    span = PER * CAP
    earlier = lax.broadcasted_iota(jnp.int32, (span, span), 0) < lax.broadcasted_iota(jnp.int32, (span, span), 1)
    my_group = me // PER
    for chunk in range(groups):
        for k in range(chunk * PER, (chunk + 1) * PER):
            if k == 0:
                copies[k].wait()
            else:
                copies[k].wait_recv()
            arrived = pl.ds(flip(me, k, n), 1)
            wide = got[arrived].reshape(SEND, width).astype(jnp.float32)
            scale = lax.rsqrt(jnp.sum(wide * wide, axis=1, keepdims=True) + 1e-06)
            scale = jnp.where(wide[:, :1] < EMPTY / 2, scale, 1.0)
            got[arrived] = (wide * scale).astype(jnp.bfloat16).reshape(1, SEND, width)
        new = flip(my_group, chunk, groups)
        for other in range(chunk + 1):
            old = flip(my_group, other, groups)
            if other == chunk:
                low, high = new, new
            else:
                top = 1 << ((chunk ^ other).bit_length() - 1)
                later = (new // top) % 2
                low = new * (1 - later) + old * later
                high = new * later + old * (1 - later)
            for c in range(CL_DEV):
                part = pl.ds(c * CAP, CAP)
                keys = got[pl.ds(low * PER, PER), part, :].reshape(span, width)
                query = got[pl.ds(high * PER, PER), part, :].reshape(span, width)
                scores = lax.dot_general(
                    keys, query, (((1,), (1,)), ((), ())), preferred_element_type=jnp.float32
                )
                keep = keys[:, :1].astype(jnp.float32) < EMPTY / 2
                if other == chunk:
                    keep = keep & earlier
                best = jnp.max(jnp.where(keep, scores, -1.0), axis=0, keepdims=True)
                line = pl.ds(high, 1)
                mine[line, c, :] = jnp.maximum(mine[line, c, :], best)

    returns = []
    for k in reversed(range(1, n)):
        peer = flip(me, k, n)
        copy = pltpu.make_async_remote_copy(
            src_ref=mine.at[peer // PER],
            dst_ref=back.at[me],
            send_sem=bsend_sem.at[k],
            recv_sem=brecv_sem.at[k],
            device_id=(group, peer),
            device_id_type=MESH,
        )
        copy.start()
        returns.append(copy)
    own = pltpu.make_async_copy(mine.at[my_group], back.at[me], own_sem)
    own.start()
    own.wait()
    for k in range(1, n):
        copies[k].wait_send()
    for copy in returns:
        copy.wait()

    lane = (me % PER) * CAP
    home = lax.broadcasted_iota(jnp.int32, (n, rows), 0) * CL_DEV
    spread = jnp.zeros((128, rows), jnp.float32)
    for c in range(CL_DEV):
        table = back[:, c, :]
        spread = spread + lax.dot_general(
            table,
            ((home + c) == label).astype(jnp.float32),
            (((0,), (0,)), ((), ())),
            preferred_element_type=jnp.float32,
            precision=lax.Precision.HIGHEST,
        )
    place = lax.broadcasted_iota(jnp.int32, (128, rows), 0) == (rank + lane)
    out_ref[...] = jnp.sum(jnp.where(place, spread, 0.0), axis=0, keepdims=True)


def solution(mesh):
    n = mesh.shape["dp"]

    def local(embeddings, labels):
        rows, width = embeddings.shape
        best = pl.pallas_call(
            functools.partial(kernel, n, rows),
            out_shape=jax.ShapeDtypeStruct((1, rows), jnp.float32),
            in_specs=[pl.BlockSpec(memory_space=pltpu.VMEM)] * 2,
            out_specs=pl.BlockSpec(memory_space=pltpu.VMEM),
            scratch_shapes=[
                pltpu.VMEM((n * SEND, width), jnp.bfloat16),
                pltpu.VMEM((n, SEND, width), jnp.bfloat16),
                pltpu.VMEM((n // PER, CL_DEV, PER * CAP), jnp.float32),
                pltpu.VMEM((n, CL_DEV, PER * CAP), jnp.float32),
                pltpu.SemaphoreType.DMA((n,)),
                pltpu.SemaphoreType.DMA((n,)),
                pltpu.SemaphoreType.DMA((n,)),
                pltpu.SemaphoreType.DMA((n,)),
                pltpu.SemaphoreType.DMA,
            ],
            compiler_params=pltpu.CompilerParams(
                collective_id=0, has_side_effects=True, vmem_limit_bytes=56 * 1024 * 1024
            ),
        )(embeddings, labels.reshape(1, rows))
        return jnp.maximum(best.reshape(rows), -1.0)

    in_specs = (P(("groups", "dp"), None), P(("groups", "dp")))
    return jax.shard_map(local, mesh=mesh, in_specs=in_specs, out_specs=P(("groups", "dp")), check_vma=False)
```
